32 devices in a mesh: seq: 8 (over z, y), head: 4 (over x, core).
Axes of the slice: x: 2, y: 2, z: 4, core: 2. Of those that a mesh axis runs over, the one named last changes fastest.
Arguments:
- queries: bfloat16 [2048, 3072], P('seq', 'head'), may hold values from -8 to 8
- key_states: bfloat16 [2048, 3072], P('seq', 'head'), may hold values from -8 to 8
- value_states: bfloat16 [2048, 3072], P('seq', 'head'), may hold values from -12 to 12
- level_offsets: int32 [3, 24], P(None, 'head'), may hold values from 0 to 31
- out_weight: bfloat16 [3072, 5120], P(None, 'head'), may hold values from -0.109375 to 0.109375
Outputs:
- layer_output: bfloat16 [2048, 5120], P('seq', 'head')
The draws below stay inside these ranges and needn't reach their ends.
All inputs are finite; a program needn't handle non-finite values.
Results may differ from the reference program's by a relative error of at most 0.0057.
Values may be sent and summed in bfloat16 or wider, within the bound.
A program may use at most 64 MiB of HBM per device.

```python
import jax
import jax.numpy as jnp
from jax import lax

D = 5120
HD = 128
HEADS = 24
LEVELS = 3
RATE_MID = 8
RATE_TOP = 32
SEG_ROWS = 1024
TOK_DEV = 256
TOKENS = 2048
N_SEQ = 8


def paired_states(key):
    columns = HEADS * HD
    query_rows = 1.3 * jax.random.normal(jax.random.fold_in(key, 11), (TOKENS, columns), jnp.float32)
    key_rows = 1.3 * jax.random.normal(jax.random.fold_in(key, 12), (TOKENS, columns), jnp.float32)
    return (jnp.clip(query_rows, -8.0, 8.0), jnp.clip(key_rows, -8.0, 8.0))


def draw_queries(key, part):
    return paired_states(key)[0].astype(jnp.bfloat16)


def draw_key_states(key, part):
    return paired_states(key)[1].astype(jnp.bfloat16)


def set_ends(array, key, low, top_value):
    place = [jax.random.randint(jax.random.fold_in(key, axis), (), 0, length) for axis, length in enumerate(array.shape)]
    widest = array.shape.index(max(array.shape))
    beside = place[:widest] + [(place[widest] + 1) % array.shape[widest]] + place[widest + 1:]
    return array.at[tuple(place)].set(low).at[tuple(beside)].set(top_value)


def steps_of(rng, extent, split, low, top_value):
    factor_of, own = 1.0, jax.random.fold_in(rng, 6)
    for axis_at, parts in split:
        heights = jnp.exp(jax.random.uniform(jax.random.fold_in(own, axis_at), (parts,), jnp.float32, low / len(split), top_value / len(split)))
        factor_of = factor_of * jnp.repeat(heights, extent[axis_at] // parts).reshape([-1 if axis == axis_at else 1 for axis in range(len(extent))])
    return factor_of


def noise(stream_key, extent, width, reach, shards=(), kind=jnp.bfloat16):
    values = width * jax.random.normal(stream_key, extent, jnp.float32)
    if shards:
        values = values * steps_of(stream_key, extent, shards, -0.22, 0.18)
    return jnp.clip(values, -reach, reach).astype(kind)


def setup_inputs(seed: int = 0) -> dict:
    key_of = jax.random.split(jax.random.key(seed), 6)
    queries = draw_queries(jax.random.fold_in(key_of[5], 71), 0)
    key_states = draw_key_states(jax.random.fold_in(key_of[5], 71), 0)
    value_states = noise(key_of[2], (TOKENS, HEADS * HD), 2.0, 12.0, ((0, 8), (1, 4)))
    level_offsets = set_ends(jax.random.randint(key_of[3], (LEVELS, HEADS), 0, RATE_TOP), jax.random.fold_in(key_of[3], 1), 0, RATE_TOP - 1).astype(jnp.int32)
    out_weight = noise(key_of[4], (HEADS * HD, D), (HEADS * HD) ** -0.5, 0.109375, ((1, 4),))
    return {"queries": queries, "key_states": key_states, "value_states": value_states, "level_offsets": level_offsets, "out_weight": out_weight}


NEG_FILL = -1e30


def spread_back(level_out, level_lse, offset, spacing):
    picked = jnp.arange(spacing, dtype=jnp.int32) == offset
    full_out = (level_out[:, None, :] * picked.astype(level_out.dtype)[None, :, None]).reshape(-1, level_out.shape[1])
    full_lse = jnp.where(picked[None, :], level_lse[:, None], NEG_FILL).reshape(-1)
    return full_out, full_lse


def head_result(inputs):
    query_head, key_head, value_head, offset_head = inputs
    scale_factor = HD ** -0.5
    level_outs = []
    level_lses = []
    for level_no, spacing in enumerate((1, RATE_MID, RATE_TOP)):
        span_devices = min(SEG_ROWS * spacing // TOK_DEV, N_SEQ)
        seg_rows = span_devices * TOK_DEV // spacing
        offset = (offset_head[level_no] % spacing).astype(jnp.int32)

        def pick_level(full_rows):
            grouped = full_rows.reshape(TOKENS // spacing, spacing, HD)
            chosen = lax.dynamic_index_in_dim(grouped, offset, 1, keepdims=False)
            return chosen.reshape(-1, seg_rows, HD).astype(jnp.float32)

        query_rows = pick_level(query_head)
        key_rows = pick_level(key_head)
        value_rows = pick_level(value_head)
        scores = jnp.einsum("sqd,skd->sqk", query_rows, key_rows, precision=lax.Precision.HIGHEST) * scale_factor
        causal = jnp.tril(jnp.ones((seg_rows, seg_rows), dtype=bool))
        scores = jnp.where(causal[None], scores, NEG_FILL)
        highest = jnp.max(scores, axis=2, keepdims=True)
        weights = jnp.exp(scores - highest)
        totals = jnp.sum(weights, axis=2, keepdims=True)
        shares = (weights / totals).astype(jnp.bfloat16).astype(jnp.float32)
        level_out = jnp.einsum("sqk,skd->sqd", shares, value_rows, precision=lax.Precision.HIGHEST).reshape(-1, HD)
        level_lse = (highest + jnp.log(totals)).reshape(-1)
        full_out, full_lse = spread_back(level_out, level_lse, offset, spacing)
        level_outs.append(full_out)
        level_lses.append(full_lse)
    lse_stack = jnp.stack(level_lses)
    level_top = jnp.max(lse_stack, axis=0)
    level_weights = jnp.exp(lse_stack - level_top[None])
    mixed_heads = jnp.sum(level_weights[:, :, None] * jnp.stack(level_outs), axis=0) / jnp.sum(level_weights, axis=0)[:, None]
    return mixed_heads.astype(jnp.bfloat16)


def reference(queries, key_states, value_states, level_offsets, out_weight):
    def by_head(matrix):
        return matrix.reshape(TOKENS, HEADS, HD).transpose(1, 0, 2)

    mixed = lax.map(head_result, (by_head(queries), by_head(key_states), by_head(value_states), level_offsets.T))
    heads_out = mixed.transpose(1, 0, 2).reshape(TOKENS, HEADS * HD)
    return jnp.dot(heads_out, out_weight, preferred_element_type=jnp.float32).astype(jnp.bfloat16)
```

```python
import functools

import jax
import jax.numpy as jnp
from jax import lax
from jax.experimental import pallas as pl
from jax.experimental.pallas import tpu as pltpu
from jax.sharding import PartitionSpec as P

RATE_MID = 8
RATE_TOP = 32
SEG_ROWS = 1024


NEG_FILL = -1e30


def push_segment(own, slots, sends, recvs, position, span, me):
    def to_later(by):
        return pltpu.make_async_remote_copy(
            src_ref=own,
            dst_ref=slots.at[position],
            send_sem=sends.at[by],
            recv_sem=recvs.at[by],
            device_id={"seq": me + by},
            device_id_type=pl.DeviceIdType.MESH,
        )

    def from_earlier(by):
        return pltpu.make_async_remote_copy(
            src_ref=own,
            dst_ref=slots.at[position - by],
            send_sem=sends.at[by],
            recv_sem=recvs.at[by],
            device_id={"seq": me - by},
            device_id_type=pl.DeviceIdType.MESH,
        )

    def start():
        @pl.loop(1, span)
        def _(by):
            @pl.when(position + by < span)
            def _():
                to_later(by).start()

    def finish():
        @pl.loop(1, span)
        def _(by):
            @pl.when(position >= by)
            def _():
                from_earlier(by).wait_recv()

            @pl.when(position + by < span)
            def _():
                to_later(by).wait_send()

    def fill():
        slots[position] = own[...]

        @pl.loop(1, span)
        def _(by):
            @pl.when(position + by < span)
            def _():
                slots[position + by] = jnp.zeros_like(own)

    return start, fill, finish


def gather_kernel(
    low_span, top_span, key_ref, value_ref, sparse_ref, keys, values, sparse, sends, recvs, sparse_sends, sparse_recvs
):
    me = lax.axis_index("seq")
    low_at, top_at = lax.rem(me, low_span), lax.rem(me, top_span)
    barrier = pltpu.get_barrier_semaphore()

    @pl.loop(1, top_span)
    def _(by):
        peer = me - top_at + lax.rem(top_at + by, top_span)
        pl.semaphore_signal(
            barrier, inc=1, device_id={"seq": peer}, device_id_type=pl.DeviceIdType.MESH
        )

    pl.semaphore_wait(barrier, top_span - 1)
    plans = (
        push_segment(sparse_ref, sparse, sparse_sends, sparse_recvs, top_at, top_span, me),
        push_segment(key_ref, keys, sends.at[0], recvs.at[0], low_at, low_span, me),
        push_segment(value_ref, values, sends.at[1], recvs.at[1], low_at, low_span, me),
    )
    for step in range(3):
        for plan in plans:
            plan[step]()


def gather_segments(key_rows, value_rows, sparse_rows, low_span, top_span):
    vmem = pl.BlockSpec(memory_space=pltpu.VMEM)
    return pl.pallas_call(
        functools.partial(gather_kernel, low_span, top_span),
        out_shape=(
            jax.ShapeDtypeStruct((low_span, *key_rows.shape), key_rows.dtype),
            jax.ShapeDtypeStruct((low_span, *value_rows.shape), value_rows.dtype),
            jax.ShapeDtypeStruct((top_span, *sparse_rows.shape), sparse_rows.dtype),
        ),
        in_specs=[vmem] * 3,
        out_specs=(vmem,) * 3,
        scratch_shapes=[
            pltpu.SemaphoreType.DMA((2, low_span)),
            pltpu.SemaphoreType.DMA((2, low_span)),
            pltpu.SemaphoreType.DMA((top_span,)),
            pltpu.SemaphoreType.DMA((top_span,)),
        ],
        compiler_params=pltpu.CompilerParams(
            collective_id=0, has_side_effects=True, vmem_limit_bytes=40 * 2**20
        ),
    )(key_rows, value_rows, sparse_rows)


def heads_kernel(peers, own, gathered, sends, recvs, relay_sends, relay_recvs):
    me = lax.axis_index("head")
    core, chips = lax.rem(me, 2), peers // 2
    other = me + 1 - 2 * core
    width = own.shape[1]
    barrier = pltpu.get_barrier_semaphore()

    def across(by):
        return lax.rem(me + 2 * by, peers)

    def behind(by):
        return lax.rem(me + peers - 2 * by, peers)

    for peer in [other] + [across(by) for by in range(1, chips)]:
        pl.semaphore_signal(
            barrier, inc=1, device_id={"head": peer}, device_id_type=pl.DeviceIdType.MESH
        )
    pl.semaphore_wait(barrier, chips)

    def columns(index):
        return gathered.at[:, pl.ds(pl.multiple_of(index * width, width), width)]

    def send(source, index, peer, send_sem, recv_sem):
        return pltpu.make_async_remote_copy(
            src_ref=source,
            dst_ref=columns(index),
            send_sem=send_sem,
            recv_sem=recv_sem,
            device_id={"head": peer},
            device_id_type=pl.DeviceIdType.MESH,
        )

    far = [send(own, me, across(by), sends.at[by], recvs.at[by]) for by in range(1, chips)]
    for copy in far:
        copy.start()
    relays = [send(own, me, other, relay_sends.at[0], relay_recvs.at[0])]
    relays[0].start()
    gathered[:, pl.ds(pl.multiple_of(me * width, width), width)] = own[...]
    for by in range(1, chips):
        source = behind(by)
        send(own, source, across(by), sends.at[by], recvs.at[by]).wait_recv()
        relay = send(columns(source), source, other, relay_sends.at[by], relay_recvs.at[by])
        relay.start()
        relays.append(relay)
    for by, relay in enumerate(relays):
        arriving = lax.rem(other + peers - 2 * by, peers)
        send(own, arriving, other, relay_sends.at[by], relay_recvs.at[by]).wait_recv()
        relay.wait_send()
    for copy in far:
        copy.wait_send()


def gather_heads(heads_out):
    peers = lax.axis_size("head")
    rows, width = heads_out.shape
    vmem = pl.BlockSpec(memory_space=pltpu.VMEM)
    return pl.pallas_call(
        functools.partial(heads_kernel, peers),
        out_shape=jax.ShapeDtypeStruct((rows, peers * width), heads_out.dtype),
        in_specs=[vmem],
        out_specs=vmem,
        scratch_shapes=[pltpu.SemaphoreType.DMA((peers // 2,))] * 4,
        compiler_params=pltpu.CompilerParams(
            collective_id=1, has_side_effects=True, vmem_limit_bytes=24 * 2**20
        ),
    )(heads_out)


def pick_rows(states, chooser, spacing):
    row_count, head_count, head_width = states.shape
    grouped = states.reshape(row_count // spacing, spacing, head_count, head_width)
    return jnp.einsum("nrhd,rh->nhd", grouped, chooser, preferred_element_type=jnp.float32).astype(
        jnp.bfloat16
    )


def attend(query_rows, key_rows, value_rows, allowed, scale_factor):
    scores = (
        jnp.einsum("qhd,khd->hqk", query_rows, key_rows, preferred_element_type=jnp.float32)
        * scale_factor
    )
    scores = jnp.where(allowed[None], scores, NEG_FILL)
    highest = jnp.max(scores, axis=2, keepdims=True)
    weights = jnp.exp(scores - highest)
    totals = jnp.sum(weights, axis=2, keepdims=True)
    shares = (weights / totals).astype(jnp.bfloat16)
    result = jnp.einsum("hqk,khd->qhd", shares, value_rows, preferred_element_type=jnp.float32)
    return (result, (highest + jnp.log(totals))[:, :, 0].T)


def segment_mask(sparse_count, span_devices, position):
    shape_pair = (sparse_count, span_devices * sparse_count)
    query_index = lax.broadcasted_iota(jnp.int32, shape_pair, 0)
    key_index = lax.broadcasted_iota(jnp.int32, shape_pair, 1)
    return key_index <= position * sparse_count + query_index


def spread_back(level_out, level_lse, chooser):
    picked = chooser.astype(jnp.float32)
    sparse_count, head_count, head_width = level_out.shape
    row_count = sparse_count * chooser.shape[0]
    full_out = (level_out[:, None, :, :] * picked[None, :, :, None]).reshape(
        row_count, head_count, head_width
    )
    full_lse = jnp.where(chooser[None], level_lse[:, None, :], NEG_FILL).reshape(
        row_count, head_count
    )
    return (full_out, full_lse)


def level_setup(query_all, key_all, value_all, offset_row, spacing):
    head_count = query_all.shape[1]
    chooser = (
        lax.broadcasted_iota(jnp.int32, (spacing, head_count), 0) == (offset_row % spacing)[None, :]
    )
    chooser_bf = chooser.astype(jnp.bfloat16)
    rows = [pick_rows(states, chooser_bf, spacing) for states in (query_all, key_all, value_all)]
    return (chooser, *rows)


def local(queries, key_states, value_states, level_offsets, out_weight):
    row_count = queries.shape[0]
    head_count = level_offsets.shape[1]
    head_width = queries.shape[1] // head_count
    scale_factor = head_width ** (-0.5)
    seq_count = lax.axis_size("seq")
    seq_index = lax.axis_index("seq")
    query_all = queries.reshape(row_count, head_count, head_width)
    key_all = key_states.reshape(row_count, head_count, head_width)
    value_all = value_states.reshape(row_count, head_count, head_width)
    spacings = (1, RATE_MID, RATE_TOP)
    spans = [min(SEG_ROWS * spacing // row_count, seq_count) for spacing in spacings]
    counts = [row_count // spacing for spacing in spacings]
    setups = [
        level_setup(query_all, key_all, value_all, level_offsets[level_no], spacings[level_no])
        for level_no in (1, 2)
    ]
    sparse_rows = jnp.concatenate(
        [rows for setup in setups for rows in setup[2:]], axis=0
    ).reshape(-1, head_count * head_width)
    keys, values, sparse = gather_segments(
        key_states, value_states, sparse_rows, spans[0], spans[2]
    )
    whole_chooser = jnp.ones((1, head_count), dtype=bool)
    levels = [(whole_chooser, query_all, keys, values)]
    first = 0
    for level_no in (1, 2):
        chooser, query_rows = setups[level_no - 1][:2]
        count, span = counts[level_no], spans[level_no]
        held = sparse
        if span < spans[2]:
            begin = (seq_index % spans[2]) // span * span
            held = lax.dynamic_slice_in_dim(sparse, begin, span, axis=0)
        levels.append(
            (chooser, query_rows, held[:, first : first + count], held[:, first + count : first + 2 * count])
        )
        first += 2 * count
    full_outs = []
    full_lses = []
    for level_no, (chooser, query_rows, key_slots, value_slots) in enumerate(levels):
        allowed = segment_mask(counts[level_no], spans[level_no], seq_index % spans[level_no])
        level_out, level_lse = attend(
            query_rows,
            key_slots.reshape(-1, head_count, head_width),
            value_slots.reshape(-1, head_count, head_width),
            allowed,
            scale_factor,
        )
        full_out, full_lse = spread_back(level_out, level_lse, chooser)
        full_outs.append(full_out)
        full_lses.append(full_lse)
    lse_stack = jnp.stack(full_lses)
    level_top = jnp.max(lse_stack, axis=0)
    level_weights = jnp.exp(lse_stack - level_top[None])
    mixed_heads = (
        jnp.sum(level_weights[..., None] * jnp.stack(full_outs), axis=0)
        / jnp.sum(level_weights, axis=0)[..., None]
    )
    heads_out = mixed_heads.astype(jnp.bfloat16).reshape(row_count, head_count * head_width)
    projected = jnp.dot(
        gather_heads(heads_out),
        out_weight,
        preferred_element_type=jnp.float32,
    )
    return projected.astype(jnp.bfloat16)


def solution(mesh):
    return jax.shard_map(
        local,
        mesh=mesh,
        in_specs=(
            P("seq", "head"),
            P("seq", "head"),
            P("seq", "head"),
            P(None, "head"),
            P(None, "head"),
        ),
        out_specs=P("seq", "head"),
        check_vma=False,
    )
```

```python
import functools

import jax
import jax.numpy as jnp
from jax import lax
from jax.experimental import pallas as pl
from jax.experimental.pallas import tpu as pltpu
from jax.sharding import PartitionSpec as P

RATE_MID = 8
RATE_TOP = 32
SEG_ROWS = 1024


NEG_FILL = -1e30


def push_segment(own, slots, sends, recvs, position, span, me):
    def to_later(by):
        return pltpu.make_async_remote_copy(
            src_ref=own,
            dst_ref=slots.at[position],
            send_sem=sends.at[by],
            recv_sem=recvs.at[by],
            device_id={"seq": me + by},
            device_id_type=pl.DeviceIdType.MESH,
        )

    def from_earlier(by):
        return pltpu.make_async_remote_copy(
            src_ref=own,
            dst_ref=slots.at[position - by],
            send_sem=sends.at[by],
            recv_sem=recvs.at[by],
            device_id={"seq": me - by},
            device_id_type=pl.DeviceIdType.MESH,
        )

    def start():
        @pl.loop(1, span)
        def _(by):
            @pl.when(position + by < span)
            def _():
                to_later(by).start()

    def finish():
        @pl.loop(1, span)
        def _(by):
            @pl.when(position >= by)
            def _():
                from_earlier(by).wait_recv()

            @pl.when(position + by < span)
            def _():
                to_later(by).wait_send()

    def fill():
        slots[position] = own[...]

        @pl.loop(1, span)
        def _(by):
            @pl.when(position + by < span)
            def _():
                slots[position + by] = jnp.zeros_like(own)

    return start, fill, lambda: None, finish


def relay_segment(own, slots, sems, position, span, me):
    odd = lax.rem(position, 2)
    pair = me + 1 - 2 * odd
    pair_at = position + 1 - 2 * odd

    def copy(source, slot, peer, row, hop):
        return pltpu.make_async_remote_copy(
            src_ref=source,
            dst_ref=slots.at[slot],
            send_sem=sems.at[row, hop],
            recv_sem=sems.at[row + 1, hop],
            device_id={"seq": peer},
            device_id_type=pl.DeviceIdType.MESH,
        )

    def start():
        @pl.when(position + 2 < span)
        def _():
            copy(own, position, me + 2, 0, 0).start()

        @pl.when(odd == 0)
        def _():
            copy(own, position, pair, 2, 0).start()

    def fill():
        slots[position] = own[...]

        @pl.loop(1, span)
        def _(by):
            @pl.when(position + by < span)
            def _():
                slots[position + by] = jnp.zeros_like(own)

    def forward():
        @pl.loop(1, span // 2)
        def _(hop):
            @pl.when(position >= 2 * hop)
            def _():
                slot = position - 2 * hop
                copy(own, slot, me - 2, 0, hop - 1).wait_recv()

                @pl.when(position + 2 < span)
                def _():
                    copy(slots.at[slot], slot, me + 2, 0, hop).start()

                copy(slots.at[slot], slot, pair, 2, hop).start()

    def finish():
        @pl.loop(0, span // 2)
        def _(hop):
            @pl.when((pair_at >= 2 * hop) & (pair_at - 2 * hop < position))
            def _():
                copy(own, pair_at - 2 * hop, pair, 2, hop).wait_recv()

            @pl.when((position >= 2 * hop) & (position + 2 < span))
            def _():
                copy(own, position - 2 * hop, me + 2, 0, hop).wait_send()

            @pl.when((position >= 2 * hop) & (position - 2 * hop < pair_at))
            def _():
                copy(own, position - 2 * hop, pair, 2, hop).wait_send()

    return start, fill, forward, finish


def gather_kernel(
    low_span, top_span, key_ref, value_ref, sparse_ref, keys, values, sparse, sends, recvs, key_sems, sparse_sems
):
    me = lax.axis_index("seq")
    low_at, top_at = lax.rem(me, low_span), lax.rem(me, top_span)
    barrier = pltpu.get_barrier_semaphore()

    @pl.loop(1, top_span)
    def _(by):
        peer = me - top_at + lax.rem(top_at + by, top_span)
        pl.semaphore_signal(
            barrier, inc=1, device_id={"seq": peer}, device_id_type=pl.DeviceIdType.MESH
        )

    pl.semaphore_wait(barrier, top_span - 1)
    plans = (
        relay_segment(sparse_ref, sparse, sparse_sems, top_at, top_span, me),
        relay_segment(key_ref, keys, key_sems, low_at, low_span, me),
        push_segment(value_ref, values, sends, recvs, low_at, low_span, me),
    )
    for step in range(4):
        for plan in plans:
            plan[step]()


def gather_segments(key_rows, value_rows, sparse_rows, low_span, top_span):
    vmem = pl.BlockSpec(memory_space=pltpu.VMEM)
    return pl.pallas_call(
        functools.partial(gather_kernel, low_span, top_span),
        out_shape=(
            jax.ShapeDtypeStruct((low_span, *key_rows.shape), key_rows.dtype),
            jax.ShapeDtypeStruct((low_span, *value_rows.shape), value_rows.dtype),
            jax.ShapeDtypeStruct((top_span, *sparse_rows.shape), sparse_rows.dtype),
        ),
        in_specs=[vmem] * 3,
        out_specs=(vmem,) * 3,
        scratch_shapes=[
            pltpu.SemaphoreType.DMA((low_span,)),
            pltpu.SemaphoreType.DMA((low_span,)),
            pltpu.SemaphoreType.DMA((4, low_span // 2)),
            pltpu.SemaphoreType.DMA((4, top_span // 2)),
        ],
        compiler_params=pltpu.CompilerParams(
            collective_id=0, has_side_effects=True, vmem_limit_bytes=40 * 2**20
        ),
    )(key_rows, value_rows, sparse_rows)


def heads_kernel(peers, own, gathered, sends, recvs, relay_sends, relay_recvs):
    me = lax.axis_index("head")
    core, chips = lax.rem(me, 2), peers // 2
    other = me + 1 - 2 * core
    width = own.shape[1]
    barrier = pltpu.get_barrier_semaphore()

    def across(by):
        return lax.rem(me + 2 * by, peers)

    def behind(by):
        return lax.rem(me + peers - 2 * by, peers)

    for peer in [other] + [across(by) for by in range(1, chips)]:
        pl.semaphore_signal(
            barrier, inc=1, device_id={"head": peer}, device_id_type=pl.DeviceIdType.MESH
        )
    pl.semaphore_wait(barrier, chips)

    def columns(index):
        return gathered.at[:, pl.ds(pl.multiple_of(index * width, width), width)]

    def send(source, index, peer, send_sem, recv_sem):
        return pltpu.make_async_remote_copy(
            src_ref=source,
            dst_ref=columns(index),
            send_sem=send_sem,
            recv_sem=recv_sem,
            device_id={"head": peer},
            device_id_type=pl.DeviceIdType.MESH,
        )

    far = [send(own, me, across(by), sends.at[by], recvs.at[by]) for by in range(1, chips)]
    for copy in far:
        copy.start()
    relays = [send(own, me, other, relay_sends.at[0], relay_recvs.at[0])]
    relays[0].start()
    gathered[:, pl.ds(pl.multiple_of(me * width, width), width)] = own[...]
    for by in range(1, chips):
        source = behind(by)
        send(own, source, across(by), sends.at[by], recvs.at[by]).wait_recv()
        relay = send(columns(source), source, other, relay_sends.at[by], relay_recvs.at[by])
        relay.start()
        relays.append(relay)
    for by, relay in enumerate(relays):
        arriving = lax.rem(other + peers - 2 * by, peers)
        send(own, arriving, other, relay_sends.at[by], relay_recvs.at[by]).wait_recv()
        relay.wait_send()
    for copy in far:
        copy.wait_send()


def gather_heads(heads_out):
    peers = lax.axis_size("head")
    rows, width = heads_out.shape
    vmem = pl.BlockSpec(memory_space=pltpu.VMEM)
    return pl.pallas_call(
        functools.partial(heads_kernel, peers),
        out_shape=jax.ShapeDtypeStruct((rows, peers * width), heads_out.dtype),
        in_specs=[vmem],
        out_specs=vmem,
        scratch_shapes=[pltpu.SemaphoreType.DMA((peers // 2,))] * 4,
        compiler_params=pltpu.CompilerParams(
            collective_id=1, has_side_effects=True, vmem_limit_bytes=24 * 2**20
        ),
    )(heads_out)


def pick_rows(states, chooser, spacing):
    row_count, head_count, head_width = states.shape
    grouped = states.reshape(row_count // spacing, spacing, head_count, head_width)
    return jnp.einsum("nrhd,rh->nhd", grouped, chooser, preferred_element_type=jnp.float32).astype(
        jnp.bfloat16
    )


def attend(query_rows, key_rows, value_rows, allowed, scale_factor):
    scores = (
        jnp.einsum("qhd,khd->hqk", query_rows, key_rows, preferred_element_type=jnp.float32)
        * scale_factor
    )
    scores = jnp.where(allowed[None], scores, NEG_FILL)
    highest = jnp.max(scores, axis=2, keepdims=True)
    weights = jnp.exp(scores - highest)
    totals = jnp.sum(weights, axis=2, keepdims=True)
    shares = (weights / totals).astype(jnp.bfloat16)
    result = jnp.einsum("hqk,khd->qhd", shares, value_rows, preferred_element_type=jnp.float32)
    return (result, (highest + jnp.log(totals))[:, :, 0].T)


def segment_mask(sparse_count, span_devices, position):
    shape_pair = (sparse_count, span_devices * sparse_count)
    query_index = lax.broadcasted_iota(jnp.int32, shape_pair, 0)
    key_index = lax.broadcasted_iota(jnp.int32, shape_pair, 1)
    return key_index <= position * sparse_count + query_index


def spread_back(level_out, level_lse, chooser):
    picked = chooser.astype(jnp.float32)
    sparse_count, head_count, head_width = level_out.shape
    row_count = sparse_count * chooser.shape[0]
    full_out = (level_out[:, None, :, :] * picked[None, :, :, None]).reshape(
        row_count, head_count, head_width
    )
    full_lse = jnp.where(chooser[None], level_lse[:, None, :], NEG_FILL).reshape(
        row_count, head_count
    )
    return (full_out, full_lse)


def level_setup(query_all, key_all, value_all, offset_row, spacing):
    head_count = query_all.shape[1]
    chooser = (
        lax.broadcasted_iota(jnp.int32, (spacing, head_count), 0) == (offset_row % spacing)[None, :]
    )
    chooser_bf = chooser.astype(jnp.bfloat16)
    rows = [pick_rows(states, chooser_bf, spacing) for states in (query_all, key_all, value_all)]
    return (chooser, *rows)


def local(queries, key_states, value_states, level_offsets, out_weight):
    row_count = queries.shape[0]
    head_count = level_offsets.shape[1]
    head_width = queries.shape[1] // head_count
    scale_factor = head_width ** (-0.5)
    seq_count = lax.axis_size("seq")
    seq_index = lax.axis_index("seq")
    query_all = queries.reshape(row_count, head_count, head_width)
    key_all = key_states.reshape(row_count, head_count, head_width)
    value_all = value_states.reshape(row_count, head_count, head_width)
    spacings = (1, RATE_MID, RATE_TOP)
    spans = [min(SEG_ROWS * spacing // row_count, seq_count) for spacing in spacings]
    counts = [row_count // spacing for spacing in spacings]
    setups = [
        level_setup(query_all, key_all, value_all, level_offsets[level_no], spacings[level_no])
        for level_no in (1, 2)
    ]
    sparse_rows = jnp.concatenate(
        [rows for setup in setups for rows in setup[2:]], axis=0
    ).reshape(-1, head_count * head_width)
    keys, values, sparse = gather_segments(
        key_states, value_states, sparse_rows, spans[0], spans[2]
    )
    whole_chooser = jnp.ones((1, head_count), dtype=bool)
    levels = [(whole_chooser, query_all, keys, values)]
    first = 0
    for level_no in (1, 2):
        chooser, query_rows = setups[level_no - 1][:2]
        count, span = counts[level_no], spans[level_no]
        held = sparse
        if span < spans[2]:
            begin = (seq_index % spans[2]) // span * span
            held = lax.dynamic_slice_in_dim(sparse, begin, span, axis=0)
        levels.append(
            (chooser, query_rows, held[:, first : first + count], held[:, first + count : first + 2 * count])
        )
        first += 2 * count
    full_outs = []
    full_lses = []
    for level_no, (chooser, query_rows, key_slots, value_slots) in enumerate(levels):
        allowed = segment_mask(counts[level_no], spans[level_no], seq_index % spans[level_no])
        level_out, level_lse = attend(
            query_rows,
            key_slots.reshape(-1, head_count, head_width),
            value_slots.reshape(-1, head_count, head_width),
            allowed,
            scale_factor,
        )
        full_out, full_lse = spread_back(level_out, level_lse, chooser)
        full_outs.append(full_out)
        full_lses.append(full_lse)
    lse_stack = jnp.stack(full_lses)
    level_top = jnp.max(lse_stack, axis=0)
    level_weights = jnp.exp(lse_stack - level_top[None])
    mixed_heads = (
        jnp.sum(level_weights[..., None] * jnp.stack(full_outs), axis=0)
        / jnp.sum(level_weights, axis=0)[..., None]
    )
    heads_out = mixed_heads.astype(jnp.bfloat16).reshape(row_count, head_count * head_width)
    projected = jnp.dot(
        gather_heads(heads_out),
        out_weight,
        preferred_element_type=jnp.float32,
    )
    return projected.astype(jnp.bfloat16)


def solution(mesh):
    return jax.shard_map(
        local,
        mesh=mesh,
        in_specs=(
            P("seq", "head"),
            P("seq", "head"),
            P("seq", "head"),
            P(None, "head"),
            P(None, "head"),
        ),
        out_specs=P("seq", "head"),
        check_vma=False,
    )
```

```python
import functools

import jax
import jax.numpy as jnp
from jax import lax
from jax.experimental import pallas as pl
from jax.experimental.pallas import tpu as pltpu
from jax.sharding import PartitionSpec as P

RATE_MID = 8
RATE_TOP = 32
SEG_ROWS = 1024


NEG_FILL = -1e30


def push_segment(own, slots, sends, recvs, position, span, me):
    def to_later(by):
        return pltpu.make_async_remote_copy(
            src_ref=own,
            dst_ref=slots.at[position],
            send_sem=sends.at[by],
            recv_sem=recvs.at[by],
            device_id={"seq": me + by},
            device_id_type=pl.DeviceIdType.MESH,
        )

    def from_earlier(by):
        return pltpu.make_async_remote_copy(
            src_ref=own,
            dst_ref=slots.at[position - by],
            send_sem=sends.at[by],
            recv_sem=recvs.at[by],
            device_id={"seq": me - by},
            device_id_type=pl.DeviceIdType.MESH,
        )

    def start():
        @pl.loop(1, span)
        def _(by):
            @pl.when(position + by < span)
            def _():
                to_later(by).start()

    def finish():
        @pl.loop(1, span)
        def _(by):
            @pl.when(position >= by)
            def _():
                from_earlier(by).wait_recv()

            @pl.when(position + by < span)
            def _():
                to_later(by).wait_send()

    def fill():
        slots[position] = own[...]

        @pl.loop(1, span)
        def _(by):
            @pl.when(position + by < span)
            def _():
                slots[position + by] = jnp.zeros_like(own)

    return start, fill, lambda: None, finish


def relay_segment(own, slots, sems, position, span, me):
    odd = lax.rem(position, 2)
    pair = me + 1 - 2 * odd
    pair_at = position + 1 - 2 * odd

    def copy(source, slot, peer, row, hop):
        return pltpu.make_async_remote_copy(
            src_ref=source,
            dst_ref=slots.at[slot],
            send_sem=sems.at[row, hop],
            recv_sem=sems.at[row + 1, hop],
            device_id={"seq": peer},
            device_id_type=pl.DeviceIdType.MESH,
        )

    def start():
        @pl.when(position + 2 < span)
        def _():
            copy(own, position, me + 2, 0, 0).start()

        @pl.when(odd == 0)
        def _():
            copy(own, position, pair, 2, 0).start()

    def fill():
        slots[position] = own[...]

        @pl.loop(1, span)
        def _(by):
            @pl.when(position + by < span)
            def _():
                slots[position + by] = jnp.zeros_like(own)

    def forward():
        @pl.loop(1, span // 2)
        def _(hop):
            @pl.when(position >= 2 * hop)
            def _():
                slot = position - 2 * hop
                copy(own, slot, me - 2, 0, hop - 1).wait_recv()

                @pl.when(position + 2 < span)
                def _():
                    copy(slots.at[slot], slot, me + 2, 0, hop).start()

                copy(slots.at[slot], slot, pair, 2, hop).start()

    def finish():
        @pl.loop(0, span // 2)
        def _(hop):
            @pl.when((pair_at >= 2 * hop) & (pair_at - 2 * hop < position))
            def _():
                copy(own, pair_at - 2 * hop, pair, 2, hop).wait_recv()

            @pl.when((position >= 2 * hop) & (position + 2 < span))
            def _():
                copy(own, position - 2 * hop, me + 2, 0, hop).wait_send()

            @pl.when((position >= 2 * hop) & (position - 2 * hop < pair_at))
            def _():
                copy(own, position - 2 * hop, pair, 2, hop).wait_send()

    return start, fill, forward, finish


def gather_kernel(
    low_span, top_span, key_ref, value_ref, sparse_ref, keys, values, sparse, sends, recvs, key_sems, sparse_sems
):
    me = lax.axis_index("seq")
    low_at, top_at = lax.rem(me, low_span), lax.rem(me, top_span)
    barrier = pltpu.get_barrier_semaphore()

    @pl.loop(1, top_span)
    def _(by):
        peer = me - top_at + lax.rem(top_at + by, top_span)
        pl.semaphore_signal(
            barrier, inc=1, device_id={"seq": peer}, device_id_type=pl.DeviceIdType.MESH
        )

    pl.semaphore_wait(barrier, top_span - 1)
    plans = (
        relay_segment(sparse_ref, sparse, sparse_sems, top_at, top_span, me),
        relay_segment(key_ref, keys, key_sems, low_at, low_span, me),
        push_segment(value_ref, values, sends, recvs, low_at, low_span, me),
    )
    for step in range(4):
        for plan in plans:
            plan[step]()


def gather_segments(key_rows, value_rows, sparse_rows, low_span, top_span):
    vmem = pl.BlockSpec(memory_space=pltpu.VMEM)
    return pl.pallas_call(
        functools.partial(gather_kernel, low_span, top_span),
        out_shape=(
            jax.ShapeDtypeStruct((low_span, *key_rows.shape), key_rows.dtype),
            jax.ShapeDtypeStruct((low_span, *value_rows.shape), value_rows.dtype),
            jax.ShapeDtypeStruct((top_span, *sparse_rows.shape), sparse_rows.dtype),
        ),
        in_specs=[vmem] * 3,
        out_specs=(vmem,) * 3,
        scratch_shapes=[
            pltpu.SemaphoreType.DMA((low_span,)),
            pltpu.SemaphoreType.DMA((low_span,)),
            pltpu.SemaphoreType.DMA((4, low_span // 2)),
            pltpu.SemaphoreType.DMA((4, top_span // 2)),
        ],
        compiler_params=pltpu.CompilerParams(
            collective_id=0, has_side_effects=True, vmem_limit_bytes=40 * 2**20
        ),
    )(key_rows, value_rows, sparse_rows)


def heads_kernel(peers, own, gathered, sends, recvs, relay_sends, relay_recvs):
    me = lax.axis_index("head")
    core, chips = lax.rem(me, 2), peers // 2
    other = me + 1 - 2 * core
    width = own.shape[1]
    barrier = pltpu.get_barrier_semaphore()

    def across(by):
        return lax.rem(me + 2 * by, peers)

    def behind(by):
        return lax.rem(me + peers - 2 * by, peers)

    for peer in [other] + [across(by) for by in range(1, chips)]:
        pl.semaphore_signal(
            barrier, inc=1, device_id={"head": peer}, device_id_type=pl.DeviceIdType.MESH
        )
    pl.semaphore_wait(barrier, chips)

    def columns(index):
        return gathered.at[:, pl.ds(pl.multiple_of(index * width, width), width)]

    def send(source, index, peer, send_sem, recv_sem):
        return pltpu.make_async_remote_copy(
            src_ref=source,
            dst_ref=columns(index),
            send_sem=send_sem,
            recv_sem=recv_sem,
            device_id={"head": peer},
            device_id_type=pl.DeviceIdType.MESH,
        )

    far = [send(own, me, across(by), sends.at[by], recvs.at[by]) for by in range(1, chips)]
    for copy in far:
        copy.start()
    relays = [send(own, me, other, relay_sends.at[0], relay_recvs.at[0])]
    relays[0].start()
    gathered[:, pl.ds(pl.multiple_of(me * width, width), width)] = own[...]
    for by in range(1, chips):
        source = behind(by)
        send(own, source, across(by), sends.at[by], recvs.at[by]).wait_recv()
        relay = send(columns(source), source, other, relay_sends.at[by], relay_recvs.at[by])
        relay.start()
        relays.append(relay)
    for by, relay in enumerate(relays):
        arriving = lax.rem(other + peers - 2 * by, peers)
        send(own, arriving, other, relay_sends.at[by], relay_recvs.at[by]).wait_recv()
        relay.wait_send()
    for copy in far:
        copy.wait_send()


def gather_heads(heads_out):
    peers = lax.axis_size("head")
    rows, width = heads_out.shape
    vmem = pl.BlockSpec(memory_space=pltpu.VMEM)
    return pl.pallas_call(
        functools.partial(heads_kernel, peers),
        out_shape=jax.ShapeDtypeStruct((rows, peers * width), heads_out.dtype),
        in_specs=[vmem],
        out_specs=vmem,
        scratch_shapes=[pltpu.SemaphoreType.DMA((peers // 2,))] * 4,
        compiler_params=pltpu.CompilerParams(
            collective_id=1, has_side_effects=True, vmem_limit_bytes=24 * 2**20
        ),
    )(heads_out)


def pick_rows(states, chooser, spacing):
    row_count, head_count, head_width = states.shape
    grouped = states.reshape(row_count // spacing, spacing, head_count, head_width)
    return jnp.einsum("nrhd,rh->nhd", grouped, chooser, preferred_element_type=jnp.float32).astype(
        jnp.bfloat16
    )


def attend(query_rows, key_rows, value_rows, allowed, scale_factor):
    scores = (
        jnp.einsum("qhd,khd->hqk", query_rows, key_rows, preferred_element_type=jnp.float32)
        * scale_factor
    )
    scores = jnp.where(allowed[None], scores, NEG_FILL)
    highest = jnp.max(scores, axis=2, keepdims=True)
    weights = jnp.exp(scores - highest)
    totals = jnp.sum(weights, axis=2, keepdims=True)
    shares = (weights / totals).astype(jnp.bfloat16)
    result = jnp.einsum("hqk,khd->qhd", shares, value_rows, preferred_element_type=jnp.float32)
    return (result, (highest + jnp.log(totals))[:, :, 0].T)


def dense_kernel(scale_factor, position_ref, query_ref, key_ref, value_ref, out_ref, lse_ref):
    rows, held = query_ref.shape[0], key_ref.shape[0]
    scores = lax.dot_general(
        query_ref[...], key_ref[...], (((1,), (1,)), ((), ())), preferred_element_type=jnp.float32
    )
    query_index = lax.broadcasted_iota(jnp.int32, (rows, held), 0)
    key_index = lax.broadcasted_iota(jnp.int32, (rows, held), 1)
    allowed = key_index <= position_ref[0] * rows + query_index
    scores = jnp.where(allowed, scores * scale_factor, NEG_FILL)
    highest = jnp.max(scores, axis=1, keepdims=True)
    weights = jnp.exp(scores - highest)
    totals = jnp.sum(weights, axis=1, keepdims=True)
    shares = (weights / totals).astype(jnp.bfloat16)
    out_ref[...] = jnp.dot(shares, value_ref[...], preferred_element_type=jnp.float32)
    lse_ref[...] = jnp.broadcast_to(highest + jnp.log(totals), lse_ref.shape)


def attend_dense(position, queries, keys, values, head_count, scale_factor):
    rows, columns = queries.shape
    width, held = columns // head_count, keys.shape[0]
    small = pl.BlockSpec((rows, width), lambda head: (0, head))
    large = pl.BlockSpec((held, width), lambda head: (0, head))
    out, lse = pl.pallas_call(
        functools.partial(dense_kernel, scale_factor),
        grid=(head_count,),
        out_shape=(jax.ShapeDtypeStruct(queries.shape, jnp.float32),) * 2,
        in_specs=[pl.BlockSpec(memory_space=pltpu.SMEM), small, large, large],
        out_specs=(small, small),
        compiler_params=pltpu.CompilerParams(vmem_limit_bytes=32 * 2**20),
    )(position.reshape(1), queries, keys, values)
    by_head = (rows, head_count, width)
    return out.reshape(by_head), lse.reshape(by_head)[:, :, 0]


def segment_mask(sparse_count, span_devices, position):
    shape_pair = (sparse_count, span_devices * sparse_count)
    query_index = lax.broadcasted_iota(jnp.int32, shape_pair, 0)
    key_index = lax.broadcasted_iota(jnp.int32, shape_pair, 1)
    return key_index <= position * sparse_count + query_index


def spread_back(level_out, level_lse, chooser):
    picked = chooser.astype(jnp.float32)
    sparse_count, head_count, head_width = level_out.shape
    row_count = sparse_count * chooser.shape[0]
    full_out = (level_out[:, None, :, :] * picked[None, :, :, None]).reshape(
        row_count, head_count, head_width
    )
    full_lse = jnp.where(chooser[None], level_lse[:, None, :], NEG_FILL).reshape(
        row_count, head_count
    )
    return (full_out, full_lse)


def level_setup(query_all, key_all, value_all, offset_row, spacing):
    head_count = query_all.shape[1]
    chooser = (
        lax.broadcasted_iota(jnp.int32, (spacing, head_count), 0) == (offset_row % spacing)[None, :]
    )
    chooser_bf = chooser.astype(jnp.bfloat16)
    rows = [pick_rows(states, chooser_bf, spacing) for states in (query_all, key_all, value_all)]
    return (chooser, *rows)


def local(queries, key_states, value_states, level_offsets, out_weight):
    row_count = queries.shape[0]
    head_count = level_offsets.shape[1]
    head_width = queries.shape[1] // head_count
    scale_factor = head_width ** (-0.5)
    seq_count = lax.axis_size("seq")
    seq_index = lax.axis_index("seq")
    query_all = queries.reshape(row_count, head_count, head_width)
    key_all = key_states.reshape(row_count, head_count, head_width)
    value_all = value_states.reshape(row_count, head_count, head_width)
    spacings = (1, RATE_MID, RATE_TOP)
    spans = [min(SEG_ROWS * spacing // row_count, seq_count) for spacing in spacings]
    counts = [row_count // spacing for spacing in spacings]
    setups = [
        level_setup(query_all, key_all, value_all, level_offsets[level_no], spacings[level_no])
        for level_no in (1, 2)
    ]
    sparse_rows = jnp.concatenate(
        [rows for setup in setups for rows in setup[2:]], axis=0
    ).reshape(-1, head_count * head_width)
    keys, values, sparse = gather_segments(
        key_states, value_states, sparse_rows, spans[0], spans[2]
    )
    columns = queries.shape[1]
    dense_out, dense_lse = attend_dense(
        seq_index % spans[0],
        queries,
        keys.reshape(-1, columns),
        values.reshape(-1, columns),
        head_count,
        scale_factor,
    )
    levels = []
    first = 0
    for level_no in (1, 2):
        chooser, query_rows = setups[level_no - 1][:2]
        count, span = counts[level_no], spans[level_no]
        held = sparse
        if span < spans[2]:
            begin = (seq_index % spans[2]) // span * span
            held = lax.dynamic_slice_in_dim(sparse, begin, span, axis=0)
        levels.append(
            (chooser, query_rows, held[:, first : first + count], held[:, first + count : first + 2 * count])
        )
        first += 2 * count
    full_outs = [dense_out]
    full_lses = [dense_lse]
    for level_no, (chooser, query_rows, key_slots, value_slots) in enumerate(levels, 1):
        allowed = segment_mask(counts[level_no], spans[level_no], seq_index % spans[level_no])
        level_out, level_lse = attend(
            query_rows,
            key_slots.reshape(-1, head_count, head_width),
            value_slots.reshape(-1, head_count, head_width),
            allowed,
            scale_factor,
        )
        full_out, full_lse = spread_back(level_out, level_lse, chooser)
        full_outs.append(full_out)
        full_lses.append(full_lse)
    lse_stack = jnp.stack(full_lses)
    level_top = jnp.max(lse_stack, axis=0)
    level_weights = jnp.exp(lse_stack - level_top[None])
    mixed_heads = (
        jnp.sum(level_weights[..., None] * jnp.stack(full_outs), axis=0)
        / jnp.sum(level_weights, axis=0)[..., None]
    )
    heads_out = mixed_heads.astype(jnp.bfloat16).reshape(row_count, head_count * head_width)
    projected = jnp.dot(
        gather_heads(heads_out),
        out_weight,
        preferred_element_type=jnp.float32,
    )
    return projected.astype(jnp.bfloat16)


def solution(mesh):
    return jax.shard_map(
        local,
        mesh=mesh,
        in_specs=(
            P("seq", "head"),
            P("seq", "head"),
            P("seq", "head"),
            P(None, "head"),
            P(None, "head"),
        ),
        out_specs=P("seq", "head"),
        check_vma=False,
    )
```
